512 devices in a mesh: fsdp: 32 (over z, core), rep: 16 (over y, x).
Axes of the slice: x: 4, y: 4, z: 16, core: 2. Of those that a mesh axis runs over, the one named last changes fastest.
Arguments:
- grads: bfloat16 [96, 16, 64, 1024], P(None, 'rep', 'fsdp'), may hold values from -4 to 4
- assignment: int32 [96], replicated, may hold values from 0 to 95, each once
- extents: int32 [96, 2], replicated, may hold values from 256 to 1024, as said below
- factor_left: float32 [96, 1024, 1024], P('fsdp', 'rep')
- factor_right: float32 [96, 1024, 1024], P('fsdp', 'rep')
- root_left: bfloat16 [96, 1024, 1024], P('fsdp', 'rep'), as said below
- root_right: bfloat16 [96, 1024, 1024], P('fsdp', 'rep'), as said below
Outputs:
- update: bfloat16 [96, 16, 64, 1024], P(None, 'rep', 'fsdp')
- new_left: float32 [96, 1024, 1024], P('fsdp', 'rep')
- new_right: float32 [96, 1024, 1024], P('fsdp', 'rep')
The draws below stay inside these ranges and needn't reach their ends.
Inputs may be any that keep to these rules, and one draw needn't show every extreme that they name: `assignment`: each block stands in exactly one owner slot. `extents`: block 0 is full; the last block is cut in its rows; other blocks are full or cut at the edge. Each block of root_right is symmetric. Each block of root_left is symmetric.
All inputs are finite; a program needn't handle non-finite values.
Results may differ from the reference program's by a relative error of at most 0.0049.
Values may be sent and summed in bfloat16 or wider, within the bound.
A program may use at most 64 MiB of HBM per device.

```python
import jax
import jax.numpy as jnp
from jax import lax

BS = 1024
NB = 96
GROUPS = 16
RW = 64


def symmetric_noise(noise, scale):
    return (noise + jnp.swapaxes(noise, 1, 2)) * (0.70710678 * scale)


def with_diagonal(offdiag, diag):
    eye = jnp.eye(BS, dtype=jnp.float32)
    return offdiag * (1.0 - eye)[None] + eye[None] * diag[:, None, :]


def draw_extents(key, part):
    key = jax.random.fold_in(key, 11)
    key_vals, key_full, key_last = jax.random.split(key, 3)
    values = jax.random.randint(key_vals, (NB, 2), BS // 4, BS + 1)
    full_flag = jax.random.randint(key_full, (NB, 2), 0, 2)
    result = jnp.where(full_flag == 1, BS, values)
    last_rows = jax.random.randint(key_last, (), BS // 4, BS)
    result = result.at[NB - 1, 0].set(last_rows)
    result = result.at[0].set(BS)
    return result.astype(jnp.int32)


def draw_factor_left(key, part):
    key = jax.random.fold_in(key, 21)
    key_off, key_diag = jax.random.split(key)
    noise = jax.random.normal(key_off, (NB, BS, BS), jnp.float32)
    diag = jax.random.uniform(key_diag, (NB, BS), jnp.float32, 2.0, 6.0)
    return with_diagonal(symmetric_noise(noise, 0.1), diag)


def draw_factor_right(key, part):
    key = jax.random.fold_in(key, 22)
    key_off, key_diag = jax.random.split(key)
    noise = jax.random.normal(key_off, (NB, BS, BS), jnp.float32)
    diag = jax.random.uniform(key_diag, (NB, BS), jnp.float32, 2.0, 6.0)
    return with_diagonal(symmetric_noise(noise, 0.1), diag)


def draw_root_left(key, part):
    key = jax.random.fold_in(key, 23)
    key_off, key_diag = jax.random.split(key)
    noise = jax.random.normal(key_off, (NB, BS, BS), jnp.float32)
    diag = jax.random.uniform(key_diag, (NB, BS), jnp.float32, 0.5, 1.5)
    return with_diagonal(symmetric_noise(noise, 0.3 / BS ** 0.5), diag).astype(jnp.bfloat16)


def draw_root_right(key, part):
    key = jax.random.fold_in(key, 24)
    key_off, key_diag = jax.random.split(key)
    noise = jax.random.normal(key_off, (NB, BS, BS), jnp.float32)
    diag = jax.random.uniform(key_diag, (NB, BS), jnp.float32, 0.5, 1.5)
    return with_diagonal(symmetric_noise(noise, 0.3 / BS ** 0.5), diag).astype(jnp.bfloat16)


def block_scale(rng, extent, shards, least, high):
    loudness = 1.0
    for position, shards_of in shards:
        heights = jax.random.uniform(jax.random.fold_in(jax.random.fold_in(rng, 6), position), (shards_of,), jnp.float32, least / len(shards), high / len(shards))
        loudness = loudness * jnp.repeat(jnp.exp(heights), extent[position] // shards_of).reshape((-1,) + (1,) * (len(extent) - 1 - position))
    return loudness


def centred(stream_key, extent, deviation, most, shards=(), kind=jnp.bfloat16):
    array = deviation * jax.random.normal(stream_key, extent, jnp.float32)
    if shards:
        array = array * block_scale(stream_key, extent, shards, -0.22, 0.18)
    return jnp.clip(array, -most, most).astype(kind)


def setup_inputs(seed: int = 0) -> dict:
    splits = jax.random.split(jax.random.key(seed), 8)
    return {
        "grads": centred(splits[0], (NB, GROUPS, RW, BS), 0.25, 4.0, ((1, 16), (2, 32))),
        "assignment": jax.random.permutation(splits[1], NB).astype(jnp.int32),
        "extents": draw_extents(jax.random.fold_in(splits[7], 71), 0),
        "factor_left": draw_factor_left(jax.random.fold_in(splits[7], 71), 0),
        "factor_right": draw_factor_right(jax.random.fold_in(splits[7], 71), 0),
        "root_left": draw_root_left(jax.random.fold_in(splits[7], 71), 0),
        "root_right": draw_root_right(jax.random.fold_in(splits[7], 71), 0),
    }


BETA = 0.95


def reference(grads, assignment, extents, factor_left, factor_right, root_left, root_right):
    blocks = grads.reshape(NB, BS, BS)
    slot_ext = jnp.take(extents, assignment, axis=0)
    index_line = jnp.arange(BS, dtype=jnp.int32)

    def one_slot(items):
        block_id, ext, left, right, root_l, root_r = items
        grad_block = lax.dynamic_index_in_dim(blocks, block_id, 0, keepdims=False)
        valid = (index_line[:, None] < ext[0]) & (index_line[None, :] < ext[1])
        grad_block = jnp.where(valid, grad_block, jnp.zeros_like(grad_block))
        left_term = jnp.dot(grad_block, grad_block.T, preferred_element_type=jnp.float32)
        right_term = jnp.dot(grad_block.T, grad_block, preferred_element_type=jnp.float32)
        next_left = BETA * left + (1.0 - BETA) * left_term
        next_right = BETA * right + (1.0 - BETA) * right_term
        precond_cols = jnp.dot(grad_block, root_r, preferred_element_type=jnp.float32).astype(jnp.bfloat16)
        result = jnp.dot(root_l, precond_cols, preferred_element_type=jnp.float32)
        result = jnp.where(valid, result, jnp.zeros_like(result)).astype(jnp.bfloat16)
        return next_left, next_right, result

    new_left, new_right, slot_update = lax.map(
        one_slot, (assignment, slot_ext, factor_left, factor_right, root_left, root_right))
    update = jnp.zeros((NB, BS, BS), jnp.bfloat16).at[assignment].set(slot_update)
    return update.reshape(NB, GROUPS, RW, BS), new_left, new_right
```

```python
import functools

import jax
import jax.numpy as jnp
from jax import lax
from jax.experimental import pallas as pl
from jax.experimental.pallas import tpu as pltpu
from jax.sharding import PartitionSpec as P

BETA = 0.95
MESH = pl.DeviceIdType.MESH
SIDE = 4
SLOTS = 3
RW = 64
BS = 1024
LANES = 128
F32 = jnp.float32
BF16 = jnp.bfloat16


def kernel(
    nf, tiles, asg, ext, root_l, root_r, ret, left_out, right_out,
    zin, fold_in, g_full, r_full, l_own, g_own, t_buf, u_buf, u_tiles, u_in, left_buf, right_buf, acc, perm, perm_t,
    z_send, z_recv, gf_send, gf_recv, rf_send, rf_recv, lf_send, lf_recv,
    ga_send, ga_recv, ra_send, ra_recv, u_send, u_recv, lo_send, lo_recv, ro_send, ro_recv, b_send, b_recv,
):
    tile_rows = tiles.shape[2]
    rpf = RW // nf
    me = lax.axis_index("fsdp")
    rep = lax.axis_index("rep")
    core = lax.rem(me, 2)
    y, x = rep // SIDE, lax.rem(rep, SIDE)
    fold = jnp.where(core == 0, y, x)
    ring = jnp.where(core == 0, x, y)
    fold_step = jnp.where(core == 0, SIDE, 1)
    ring_step = jnp.where(core == 0, 1, SIDE)

    def at(fold_pos, ring_pos):
        return fold_pos * fold_step + ring_pos * ring_step

    right = lax.rem(ring + 1, SIDE)
    left = lax.rem(ring + SIDE - 1, SIDE)
    across = lax.rem(ring + 2, SIDE)
    works = fold < SLOTS

    def remote(src, dst, ssem, rsem, fs, rp):
        return pltpu.make_async_remote_copy(
            src_ref=src, dst_ref=dst, send_sem=ssem, recv_sem=rsem, device_id=(fs, rp), device_id_type=MESH
        )

    def taken(ref, sem):
        pltpu.make_async_copy(ref, ref, sem).wait()

    barrier = pltpu.get_barrier_semaphore()

    def greet(d, carry):
        pl.semaphore_signal(barrier, inc=1, device_id=(lax.rem(me + d, nf), rep), device_id_type=MESH)
        return carry

    lax.fori_loop(1, nf, greet, 0)
    for d in range(1, SIDE):
        pl.semaphore_signal(barrier, inc=1, device_id=(me, at(lax.rem(fold + d, SIDE), ring)), device_id_type=MESH)
    for pos in (left, right):
        pl.semaphore_signal(barrier, inc=1, device_id=(me, at(fold, pos)), device_id_type=MESH)
    pl.semaphore_wait(barrier, nf - 1 + SIDE - 1 + 2)

    for s in range(SLOTS):
        @pl.when(fold != s)
        def _():
            remote(root_r.at[s], r_full.at[rep], rf_send.at[s], rf_recv.at[fold], me, at(s, ring)).start()
            remote(root_l.at[s], l_own.at[fold], lf_send.at[s], lf_recv.at[fold], me, at(s, ring)).start()

        @pl.when(fold == s)
        def _():
            pltpu.make_async_copy(root_r.at[s], r_full.at[rep], rf_recv.at[fold]).start()
            pltpu.make_async_copy(root_l.at[s], l_own.at[fold], lf_recv.at[fold]).start()

    def other(i):
        half = (i + 1) // 2
        return lax.rem(me + jnp.where(lax.rem(i, 2) == 1, half, nf - half), nf)

    for s in range(SLOTS):
        pltpu.make_async_copy(tiles.at[s, me], zin.at[s, me], z_recv.at[s]).start()

        def push(i, carry):
            to = other(i)
            remote(tiles.at[s, to], zin.at[s, me], z_send.at[s], z_recv.at[s], to, rep).start()
            return carry

        lax.fori_loop(1, nf, push, 0)

    size = 8 * RW
    one = lax.broadcasted_iota(jnp.int32, (size, size), 0)
    two = lax.broadcasted_iota(jnp.int32, (size, size), 1)

    def tile_place(o):
        return (lax.rem(o, RW) // rpf) * tile_rows + (o // RW) * rpf + lax.rem(o, rpf)

    perm[...] = jnp.where(two == tile_place(one), 1.0, 0.0).astype(BF16)
    perm_t[...] = jnp.where(one == tile_place(two), 1.0, 0.0).astype(BF16)

    def spread(buf, sends, recvs, f):
        g = at(f, ring)
        remote(buf.at[g], buf.at[g], sends.at[0, f], recvs.at[0, f], me, at(fold, right)).start()
        remote(buf.at[g], buf.at[g], sends.at[1, f], recvs.at[1, f], me, at(fold, left)).start()

    def pass_on(buf, sends, recvs):
        for f in range(SIDE):
            way = 0 if f < 2 else 1
            g = at(f, left if way == 0 else right)
            taken(buf.at[g], recvs.at[way, f])
            remote(buf.at[g], buf.at[g], sends.at[2, f], recvs.at[2, f], me, at(fold, right if way == 0 else left)).start()

    def rest(buf, recvs):
        for f in range(SIDE):
            way = 1 if f < 2 else 0
            taken(buf.at[at(f, right if way == 1 else left)], recvs.at[way, f])
            taken(buf.at[at(f, across)], recvs.at[2, f])

    @pl.when(works)
    def _():
        for f in range(SIDE):
            taken(r_full.at[at(f, ring)], rf_recv.at[f])
            spread(r_full, ra_send, ra_recv, f)

    slot = me * SLOTS + jnp.minimum(fold, SLOTS - 1)
    block = asg[slot]
    rows_ok = ext[2 * block]
    cols_ok = ext[2 * block + 1]

    def unpack(i, carry):
        f = lax.rem(fold + i, SIDE)
        taken(fold_in.at[f], gf_recv.at[f])
        g = at(f, ring)
        flat = jnp.dot(perm[...], fold_in[f].reshape(size, LANES), preferred_element_type=F32)
        row_ids = g * RW + lax.broadcasted_iota(jnp.int32, (RW, LANES), 0)
        col_ids = lax.broadcasted_iota(jnp.int32, (RW, LANES), 1)
        for c in range(BS // LANES):
            ok = jnp.logical_and(row_ids < rows_ok, col_ids + c * LANES < cols_ok)
            part = jnp.where(ok, flat[c * RW : (c + 1) * RW, :], 0.0).astype(BF16)
            g_full[g, :, c * LANES : (c + 1) * LANES] = part
            g_own[f, :, c * LANES : (c + 1) * LANES] = part
        spread(g_full, ga_send, ga_recv, f)
        return carry

    for s in range(SLOTS):
        taken(zin.at[s], z_recv.at[s])

        @pl.when(fold != s)
        def _():
            remote(zin.at[s], fold_in.at[fold], gf_send.at[s], gf_recv.at[fold], me, at(s, ring)).start()

        @pl.when(fold == s)
        def _():
            pltpu.make_async_copy(zin.at[s], fold_in.at[fold], gf_recv.at[fold]).start()
            lax.fori_loop(0, SIDE, unpack, 0)

        if s == 0:
            @pl.when(works)
            def _():
                pass_on(r_full, ra_send, ra_recv)
        else:
            @pl.when(fold == s - 1)
            def _():
                pass_on(g_full, ga_send, ga_recv)

    @pl.when(fold == SLOTS - 1)
    def _():
        pass_on(g_full, ga_send, ga_recv)

    width = 256
    own_rows = SIDE * RW

    def columns(j):
        return pl.ds(pl.multiple_of(j * width, width), width)

    def update_part():
        rest(g_full, ga_recv)
        for f in range(SIDE):
            taken(l_own.at[f], lf_recv.at[f])

        def t_cols(j, carry):
            t_buf[:, columns(j)] = jnp.dot(
                l_own[...].reshape(own_rows, BS), g_full[:, :, columns(j)].reshape(BS, width), preferred_element_type=F32
            ).astype(BF16)
            return carry

        lax.fori_loop(0, BS // width, t_cols, 0)
        rest(r_full, ra_recv)

        def u_cols(j, carry):
            u = jnp.dot(t_buf[...], r_full[:, :, columns(j)].reshape(BS, width), preferred_element_type=F32)
            col_ids = j * width + lax.broadcasted_iota(jnp.int32, (RW, width), 1)
            for f in range(SIDE):
                row_ids = at(f, ring) * RW + lax.broadcasted_iota(jnp.int32, (RW, width), 0)
                ok = jnp.logical_and(row_ids < rows_ok, col_ids < cols_ok)
                u_buf[f * RW : (f + 1) * RW, columns(j)] = jnp.where(ok, u[f * RW : (f + 1) * RW, :], 0.0).astype(BF16)
            return carry

        lax.fori_loop(0, BS // width, u_cols, 0)
        for f in range(SIDE):
            rows = u_buf[f * RW : (f + 1) * RW, :]
            flat = jnp.concatenate([rows[:, c * LANES : (c + 1) * LANES] for c in range(BS // LANES)], axis=0)
            u_tiles[f] = (
                jnp.dot(perm_t[...], flat, preferred_element_type=F32).astype(BF16).reshape(nf, tile_rows, LANES)
            )

            @pl.when(fold != f)
            def _():
                remote(u_tiles.at[f], u_in.at[fold], u_send.at[f], u_recv.at[fold], me, at(f, ring)).start()

            @pl.when(fold == f)
            def _():
                pltpu.make_async_copy(u_tiles.at[f], u_in.at[fold], u_recv.at[fold]).start()

    def factor_part():
        def left_cols(j, carry):
            part = lax.dot_general(
                g_own[...].reshape(own_rows, BS),
                g_full[pl.ds(j * (width // RW), width // RW)].reshape(width, BS),
                (((1,), (1,)), ((), ())),
                preferred_element_type=F32,
            )
            left_buf[:, :, columns(j)] = ((1.0 - BETA) * part).astype(BF16).reshape(SIDE, RW, width)
            return carry

        lax.fori_loop(0, BS // width, left_cols, 0)

        def home(buf, out, sends, recvs, f):
            @pl.when(fold != f)
            def _():
                remote(buf.at[f], out.at[fold], sends.at[f], recvs.at[fold], me, at(f, ring)).start()

            @pl.when(fold == f)
            def _():
                pltpu.make_async_copy(buf.at[f], out.at[fold], recvs.at[fold]).start()

        for f in range(SIDE):
            home(left_buf, left_out, lo_send, lo_recv, f)

        for f in range(SIDE):
            g = at(f, ring)
            pair = pl.ds(pl.multiple_of((g // 2) * LANES, LANES), LANES)

            def right_cols(j, carry):
                acc[...] = lax.dot_general(
                    g_full[:, :, pair].reshape(BS, LANES),
                    g_full[:, :, columns(j)].reshape(BS, width),
                    (((0,), (0,)), ((), ())),
                    preferred_element_type=F32,
                )
                mine = acc[pl.ds(pl.multiple_of(lax.rem(g, 2) * RW, RW), RW), :]
                right_buf[f, :, columns(j)] = ((1.0 - BETA) * mine).astype(BF16)
                return carry

            lax.fori_loop(0, BS // width, right_cols, 0)
            home(right_buf, right_out, ro_send, ro_recv, f)

    for s in range(SLOTS):
        pl.when(fold == s)(update_part)
        taken(u_in.at[s], u_recv.at[s])
        pltpu.make_async_copy(u_in.at[s, me], ret.at[s, me], b_recv.at[s]).start()

        def push_back(i, carry):
            to = other(i)
            remote(u_in.at[s, to], ret.at[s, me], b_send.at[s], b_recv.at[s], to, rep).start()
            return carry

        lax.fori_loop(1, nf, push_back, 0)
        pl.when(fold == s)(factor_part)

    for s in range(SLOTS):
        taken(left_out.at[s], lo_recv.at[s])
        taken(right_out.at[s], ro_recv.at[s])
        taken(ret.at[s], b_recv.at[s])
        taken(zin.at[s, pl.ds(0, nf - 1)], z_send.at[s])
        taken(u_in.at[s, pl.ds(0, nf - 1)], b_send.at[s])

        @pl.when(fold != s)
        def _():
            taken(zin.at[s], gf_send.at[s])
            taken(root_r.at[s], rf_send.at[s])
            taken(root_l.at[s], lf_send.at[s])

    @pl.when(works)
    def _():
        for f in range(SIDE):
            for way in range(3):
                taken(g_full.at[f], ga_send.at[way, f])
                taken(r_full.at[f], ra_send.at[way, f])

            @pl.when(fold != f)
            def _():
                taken(u_tiles.at[f], u_send.at[f])
                taken(left_buf.at[f], lo_send.at[f])
                taken(right_buf.at[f], ro_send.at[f])


def local(nf, grads, assignment, extents, factor_left, factor_right, root_left, root_right):
    nblocks = assignment.shape[0]
    rpf = RW // nf
    tile_rows = rpf * BS // LANES
    by_slot = assignment.reshape(nf, SLOTS).T.reshape(-1)
    ordered = grads.reshape(nblocks, rpf, BS).at[by_slot].get(mode="promise_in_bounds")
    tiles = ordered.reshape(nblocks, rpf, BS // LANES, LANES).transpose(0, 2, 1, 3)
    tiles = tiles.reshape(SLOTS, nf, tile_rows, LANES)
    dma = pltpu.SemaphoreType.DMA
    anywhere = pl.BlockSpec(memory_space=pl.ANY)
    vmem = pl.BlockSpec(memory_space=pltpu.VMEM)
    smem = pl.BlockSpec(memory_space=pltpu.SMEM)
    rows = (SLOTS, RW, BS)
    own = (SIDE, RW, BS)
    ret, left_term, right_term = pl.pallas_call(
        functools.partial(kernel, nf),
        out_shape=(
            jax.ShapeDtypeStruct((SLOTS, nf, tile_rows, LANES), BF16),
            jax.ShapeDtypeStruct(rows, BF16),
            jax.ShapeDtypeStruct(rows, BF16),
        ),
        in_specs=[vmem, smem, smem, anywhere, anywhere],
        out_specs=(anywhere, anywhere, anywhere),
        scratch_shapes=[
            pltpu.VMEM((SLOTS, nf, tile_rows, LANES), BF16),
            pltpu.VMEM((SIDE, nf, tile_rows, LANES), BF16),
            pltpu.VMEM((SIDE * SIDE, RW, BS), BF16),
            pltpu.VMEM((SIDE * SIDE, RW, BS), BF16),
            pltpu.VMEM(own, BF16),
            pltpu.VMEM(own, BF16),
            pltpu.VMEM((SIDE * RW, BS), BF16),
            pltpu.VMEM((SIDE * RW, BS), BF16),
            pltpu.VMEM((SIDE, nf, tile_rows, LANES), BF16),
            pltpu.VMEM((SLOTS, nf, tile_rows, LANES), BF16),
            pltpu.VMEM(own, BF16),
            pltpu.VMEM(own, BF16),
            pltpu.VMEM((LANES, 256), F32),
            pltpu.VMEM((8 * RW, 8 * RW), BF16),
            pltpu.VMEM((8 * RW, 8 * RW), BF16),
            dma((SLOTS,)), dma((SLOTS,)),
            dma((SLOTS,)), dma((SIDE,)),
            dma((SLOTS,)), dma((SIDE,)),
            dma((SLOTS,)), dma((SIDE,)),
            dma((3, SIDE)), dma((3, SIDE)),
            dma((3, SIDE)), dma((3, SIDE)),
            dma((SIDE,)), dma((SLOTS,)),
            dma((SIDE,)), dma((SLOTS,)),
            dma((SIDE,)), dma((SLOTS,)),
            dma((SLOTS,)), dma((SLOTS,)),
        ],
        compiler_params=pltpu.CompilerParams(
            collective_id=0, has_side_effects=True, vmem_limit_bytes=40 * 1024 * 1024
        ),
    )(tiles, assignment, extents.reshape(-1), root_left, root_right)
    new_left = BETA * factor_left + left_term.astype(F32)
    new_right = BETA * factor_right + right_term.astype(F32)
    line = jnp.arange(nblocks, dtype=jnp.int32)
    places = (line % SLOTS) * nf + line // SLOTS
    inverse = jnp.sum(jnp.where(assignment[None, :] == line[:, None], places[None, :], 0), axis=1)
    flat = ret.reshape(nblocks, BS // LANES, rpf, LANES).transpose(0, 2, 1, 3).reshape(nblocks, rpf, BS)
    update = flat.at[inverse].get(mode="promise_in_bounds").reshape(nblocks, 1, rpf, BS)
    return (update, new_left, new_right)


def solution(mesh):
    placed = (
        P(None, "rep", "fsdp", None),
        P(),
        P(),
        P("fsdp", "rep", None),
        P("fsdp", "rep", None),
        P("fsdp", "rep", None),
        P("fsdp", "rep", None),
    )
    return jax.shard_map(
        functools.partial(local, mesh.shape["fsdp"]),
        mesh=mesh,
        in_specs=placed,
        out_specs=(P(None, "rep", "fsdp", None), P("fsdp", "rep", None), P("fsdp", "rep", None)),
        check_vma=False,
    )
```

```python
import functools

import jax
import jax.numpy as jnp
from jax import lax
from jax.experimental import pallas as pl
from jax.experimental.pallas import tpu as pltpu
from jax.sharding import PartitionSpec as P

BETA = 0.95
MESH = pl.DeviceIdType.MESH
SIDE = 4
SLOTS = 3
RW = 64
BS = 1024
LANES = 128
F32 = jnp.float32
BF16 = jnp.bfloat16


def kernel(
    nf, grads, asg_in, ext_in, root_l, root_r, ret, left_out, right_out,
    asg, ext, grads_v, tiles, zin, fold_in, g_full, r_full, l_own, g_own, t_buf, u_buf, u_tiles, u_in, left_buf, right_buf, turned, g_cols,
    perm, perm_t,
    grads_sem, asg_sem, ext_sem, z_send, z_recv, gf_send, gf_recv, rf_send, rf_recv, lf_send, lf_recv,
    ga_send, ga_recv, ra_send, ra_recv, u_send, u_recv, lo_send, lo_recv, ro_send, ro_recv, b_send, b_recv,
):
    me = lax.axis_index("fsdp")
    rep = lax.axis_index("rep")
    core = lax.rem(me, 2)
    y, x = rep // SIDE, lax.rem(rep, SIDE)
    fold = jnp.where(core == 0, y, x)
    ring = jnp.where(core == 0, x, y)
    fold_step = jnp.where(core == 0, SIDE, 1)
    ring_step = jnp.where(core == 0, 1, SIDE)

    def at(fold_pos, ring_pos):
        return fold_pos * fold_step + ring_pos * ring_step

    right = lax.rem(ring + 1, SIDE)
    left = lax.rem(ring + SIDE - 1, SIDE)
    across = lax.rem(ring + 2, SIDE)
    works = fold < SLOTS

    def remote(src, dst, ssem, rsem, fs, rp):
        return pltpu.make_async_remote_copy(
            src_ref=src, dst_ref=dst, send_sem=ssem, recv_sem=rsem, device_id=(fs, rp), device_id_type=MESH
        )

    def taken(ref, sem):
        pltpu.make_async_copy(ref, ref, sem).wait()

    staged = pltpu.make_async_copy(grads, grads_v, grads_sem)
    staged.start()
    numbers = pltpu.make_async_copy(asg_in, asg, asg_sem)
    numbers.start()
    limits = pltpu.make_async_copy(ext_in, ext, ext_sem)
    limits.start()

    barrier = pltpu.get_barrier_semaphore()

    def greet(d, carry):
        pl.semaphore_signal(barrier, inc=1, device_id=(lax.rem(me + d, nf), rep), device_id_type=MESH)
        return carry

    for d in range(1, SIDE):
        pl.semaphore_signal(barrier, inc=1, device_id=(me, at(lax.rem(fold + d, SIDE), ring)), device_id_type=MESH)
    for pos in (left, right):
        pl.semaphore_signal(barrier, inc=1, device_id=(me, at(fold, pos)), device_id_type=MESH)
    lax.fori_loop(1, nf, greet, 0)
    pl.semaphore_wait(barrier, nf - 1 + SIDE - 1 + 2)

    def fold_root(root, place, sends, recvs):
        def push(s, carry):
            @pl.when(fold != s)
            def _():
                remote(root.at[s], place, sends.at[s], recvs.at[fold], me, at(s, ring)).start()

            @pl.when(fold == s)
            def _():
                pltpu.make_async_copy(root.at[s], place, recvs.at[fold]).start()

            return carry

        lax.fori_loop(0, SLOTS, push, 0)

    def other(i):
        half = (nf + 1 - i) // 2
        return lax.rem(me + jnp.where(lax.rem(i, 2) == 0, half, nf - half), nf)

    def send_tiles(s, carry):
        def push(i, carry):
            to = other(i)
            tiles[s, to] = grads_v[asg[to * SLOTS + s]]
            remote(tiles.at[s, to], zin.at[s, me], z_send.at[s], z_recv.at[s], to, rep).start()
            return carry

        lax.fori_loop(1, nf, push, 0)
        tiles[s, me] = grads_v[asg[me * SLOTS + s]]
        pltpu.make_async_copy(tiles.at[s, me], zin.at[s, me], z_recv.at[s]).start()
        return carry

    fold_root(root_r, r_full.at[rep], rf_send, rf_recv)
    staged.wait()
    numbers.wait()
    limits.wait()
    lax.fori_loop(0, SLOTS, send_tiles, 0)
    fold_root(root_l, l_own.at[fold], lf_send, lf_recv)

    one = lax.broadcasted_iota(jnp.int32, (LANES, LANES), 0)
    two = lax.broadcasted_iota(jnp.int32, (LANES, LANES), 1)

    def tile_place(o):
        return (lax.rem(o, 16) // 2) * 16 + (o // 16) * 2 + lax.rem(o, 2)

    perm[...] = jnp.where(two == tile_place(one), 1.0, 0.0).astype(BF16)
    perm_t[...] = jnp.where(one == tile_place(two), 1.0, 0.0).astype(BF16)

    def spread(buf, sends, recvs, f):
        g = at(f, ring)
        remote(buf.at[g], buf.at[g], sends.at[0, f], recvs.at[0, f], me, at(fold, right)).start()
        remote(buf.at[g], buf.at[g], sends.at[1, f], recvs.at[1, f], me, at(fold, left)).start()

    def pass_on(buf, sends, recvs):
        def push(i, carry):
            way = lax.rem(i, 2)
            f = way * 2 + i // 2
            g = at(f, jnp.where(way == 0, left, right))
            taken(buf.at[g], recvs.at[way, f])
            to = at(fold, jnp.where(way == 0, right, left))
            remote(buf.at[g], buf.at[g], sends.at[2, f], recvs.at[2, f], me, to).start()
            return carry

        lax.fori_loop(0, SIDE, push, 0)

    def rest(buf, recvs):
        def await_piece(f, carry):
            way = 1 - f // 2
            taken(buf.at[at(f, jnp.where(way == 0, left, right))], recvs.at[way, f])
            taken(buf.at[at(f, across)], recvs.at[2, f])
            return carry

        lax.fori_loop(0, SIDE, await_piece, 0)

    slot = me * SLOTS + jnp.minimum(fold, SLOTS - 1)
    block = asg[slot]
    rows_ok = ext[0, block]
    cols_ok = ext[1, block]

    def unpack(i, carry):
        f = lax.rem(fold + i, SIDE)
        taken(fold_in.at[f], gf_recv.at[f])
        g = at(f, ring)
        groups = [fold_in[f, q * 8 : (q + 1) * 8].reshape(LANES, LANES) for q in range(4)]
        flat = jnp.dot(perm[...], jnp.concatenate(groups, axis=1), preferred_element_type=F32)
        row_ids = g * RW + lax.broadcasted_iota(jnp.int32, (16, LANES), 0)
        col_ids = lax.broadcasted_iota(jnp.int32, (16, LANES), 1)
        for q in range(4):
            for c in range(BS // LANES):
                ok = jnp.logical_and(row_ids + q * 16 < rows_ok, col_ids + c * LANES < cols_ok)
                part = flat[c * 16 : (c + 1) * 16, q * LANES : (q + 1) * LANES]
                part = jnp.where(ok, part, 0.0).astype(BF16)
                g_full[g, q * 16 : (q + 1) * 16, c * LANES : (c + 1) * LANES] = part
                g_own[f, q * 16 : (q + 1) * 16, c * LANES : (c + 1) * LANES] = part
        spread(g_full, ga_send, ga_recv, f)
        return carry

    own_rows = SIDE * RW

    def update_part():
        rest(g_full, ga_recv)

        def await_left(f, carry):
            taken(l_own.at[f], lf_recv.at[f])
            return carry

        lax.fori_loop(0, SIDE, await_left, 0)
        t_buf[...] = jnp.dot(
            l_own[...].reshape(own_rows, BS), g_full[...].reshape(BS, BS), preferred_element_type=F32
        ).astype(BF16)
        rest(r_full, ra_recv)
        u = jnp.dot(t_buf[...], r_full[...].reshape(BS, BS), preferred_element_type=F32)
        col_ids = lax.broadcasted_iota(jnp.int32, (RW, BS), 1)
        for f in range(SIDE):
            row_ids = at(f, ring) * RW + lax.broadcasted_iota(jnp.int32, (RW, BS), 0)
            ok = jnp.logical_and(row_ids < rows_ok, col_ids < cols_ok)
            u_buf[f * RW : (f + 1) * RW, :] = jnp.where(ok, u[f * RW : (f + 1) * RW, :], 0.0).astype(BF16)

        def pack(i, carry):
            f = lax.rem(fold + 1 + i, SIDE)
            rows = u_buf[pl.ds(pl.multiple_of(f * RW, RW), RW), :]
            groups = [
                jnp.concatenate(
                    [rows[q * 16 : (q + 1) * 16, c * LANES : (c + 1) * LANES] for c in range(BS // LANES)], axis=0
                )
                for q in range(4)
            ]
            flat = jnp.dot(perm_t[...], jnp.concatenate(groups, axis=1), preferred_element_type=F32).astype(BF16)
            for q in range(4):
                u_tiles[f, q * 8 : (q + 1) * 8] = flat[:, q * LANES : (q + 1) * LANES].reshape(8, 16, LANES)

            @pl.when(fold != f)
            def _():
                remote(u_tiles.at[f], u_in.at[fold], u_send.at[f], u_recv.at[fold], me, at(f, ring)).start()

            @pl.when(fold == f)
            def _():
                pltpu.make_async_copy(u_tiles.at[f], u_in.at[fold], u_recv.at[fold]).start()

            return carry

        lax.fori_loop(0, SIDE, pack, 0)

    def factor_part():
        part = lax.dot_general(
            g_own[...].reshape(own_rows, BS),
            g_full[...].reshape(BS, BS),
            (((1,), (1,)), ((), ())),
            preferred_element_type=F32,
        )
        left_buf[...] = ((1.0 - BETA) * part).astype(BF16).reshape(SIDE, RW, BS)

        def home(buf, out, sends, recvs, f):
            @pl.when(fold != f)
            def _():
                remote(buf.at[f], out.at[fold], sends.at[f], recvs.at[fold], me, at(f, ring)).start()

            @pl.when(fold == f)
            def _():
                pltpu.make_async_copy(buf.at[f], out.at[fold], recvs.at[fold]).start()

        def left_home(f, carry):
            home(left_buf, left_out, lo_send, lo_recv, f)
            return carry

        lax.fori_loop(0, SIDE, left_home, 0)

        def own_columns(f, carry):
            g = at(f, ring)
            pair = pl.ds(pl.multiple_of((g // 2) * LANES, LANES), LANES)
            turned[...] = g_full[:, :, pair].reshape(BS, LANES).T
            g_cols[f] = turned[pl.ds(pl.multiple_of(lax.rem(g, 2) * RW, RW), RW), :]
            return carry

        lax.fori_loop(0, SIDE, own_columns, 0)
        part = jnp.dot(g_cols[...].reshape(own_rows, BS), g_full[...].reshape(BS, BS), preferred_element_type=F32)
        right_buf[...] = ((1.0 - BETA) * part).astype(BF16).reshape(SIDE, RW, BS)

        def right_home(f, carry):
            home(right_buf, right_out, ro_send, ro_recv, f)
            return carry

        lax.fori_loop(0, SIDE, right_home, 0)

    def send_back(s):
        taken(u_in.at[s], u_recv.at[s])

        def push_back(i, carry):
            to = other(i)
            remote(u_in.at[s, to], ret.at[s, me], b_send.at[s], b_recv.at[s], to, rep).start()
            return carry

        lax.fori_loop(1, nf, push_back, 0)
        pltpu.make_async_copy(u_in.at[s, me], ret.at[s, me], b_recv.at[s]).start()

    @pl.when(works)
    def _():
        def root_piece(f, carry):
            taken(r_full.at[at(f, ring)], rf_recv.at[f])
            spread(r_full, ra_send, ra_recv, f)
            return carry

        lax.fori_loop(0, SIDE, root_piece, 0)

    def fold_tiles(s, carry):
        taken(zin.at[s], z_recv.at[s])

        @pl.when(fold != s)
        def _():
            remote(zin.at[s], fold_in.at[fold], gf_send.at[s], gf_recv.at[fold], me, at(s, ring)).start()

        @pl.when(fold == s)
        def _():
            pltpu.make_async_copy(zin.at[s], fold_in.at[fold], gf_recv.at[fold]).start()
            lax.fori_loop(0, SIDE, unpack, 0)

        @pl.when(jnp.logical_and(works, s == 0))
        def _():
            pass_on(r_full, ra_send, ra_recv)

        return carry

    lax.fori_loop(0, SLOTS, fold_tiles, 0)

    @pl.when(works)
    def _():
        pass_on(g_full, ga_send, ga_recv)

    def turn(s, carry):
        @pl.when(jnp.logical_and(works, s == jnp.maximum(fold - 1, 0)))
        def _():
            update_part()

        send_back(s)
        pl.when(fold == s)(factor_part)
        return carry

    lax.fori_loop(0, SLOTS, turn, 0)

    def finish(s, carry):
        taken(left_out.at[s], lo_recv.at[s])
        taken(right_out.at[s], ro_recv.at[s])
        taken(ret.at[s], b_recv.at[s])
        taken(tiles.at[s, pl.ds(0, nf - 1)], z_send.at[s])
        taken(u_in.at[s, pl.ds(0, nf - 1)], b_send.at[s])

        @pl.when(fold != s)
        def _():
            taken(zin.at[s], gf_send.at[s])
            taken(root_r.at[s], rf_send.at[s])
            taken(root_l.at[s], lf_send.at[s])

        return carry

    lax.fori_loop(0, SLOTS, finish, 0)

    @pl.when(works)
    def _():
        def sent(f, carry):
            for way in range(3):
                taken(g_full.at[f], ga_send.at[way, f])
                taken(r_full.at[f], ra_send.at[way, f])

            @pl.when(fold != f)
            def _():
                taken(u_tiles.at[f], u_send.at[f])
                taken(left_buf.at[f], lo_send.at[f])
                taken(right_buf.at[f], ro_send.at[f])

            return carry

        lax.fori_loop(0, SIDE, sent, 0)


def local(nf, grads, assignment, extents, factor_left, factor_right, root_left, root_right):
    nblocks = assignment.shape[0]
    rpf = RW // nf
    tile_rows = rpf * BS // LANES
    split = grads.reshape(nblocks, rpf, BS // LANES, LANES).transpose(0, 2, 1, 3).reshape(nblocks, tile_rows, LANES)
    dma = pltpu.SemaphoreType.DMA
    anywhere = pl.BlockSpec(memory_space=pl.ANY)
    hbm = pl.BlockSpec(memory_space=pltpu.HBM)
    rows = (SLOTS, RW, BS)
    own = (SIDE, RW, BS)
    ret, left_term, right_term = pl.pallas_call(
        functools.partial(kernel, nf),
        out_shape=(
            jax.ShapeDtypeStruct((SLOTS, nf, tile_rows, LANES), BF16),
            jax.ShapeDtypeStruct(rows, BF16),
            jax.ShapeDtypeStruct(rows, BF16),
        ),
        in_specs=[hbm] * 5,
        out_specs=(anywhere, anywhere, anywhere),
        scratch_shapes=[
            pltpu.SMEM((nblocks,), jnp.int32),
            pltpu.SMEM((2, nblocks), jnp.int32),
            pltpu.VMEM((nblocks, tile_rows, LANES), BF16),
            pltpu.VMEM((SLOTS, nf, tile_rows, LANES), BF16),
            pltpu.VMEM((SLOTS, nf, tile_rows, LANES), BF16),
            pltpu.VMEM((SIDE, nf, tile_rows, LANES), BF16),
            pltpu.VMEM((SIDE * SIDE, RW, BS), BF16),
            pltpu.VMEM((SIDE * SIDE, RW, BS), BF16),
            pltpu.VMEM(own, BF16),
            pltpu.VMEM(own, BF16),
            pltpu.VMEM((SIDE * RW, BS), BF16),
            pltpu.VMEM((SIDE * RW, BS), BF16),
            pltpu.VMEM((SIDE, nf, tile_rows, LANES), BF16),
            pltpu.VMEM((SLOTS, nf, tile_rows, LANES), BF16),
            pltpu.VMEM(own, BF16),
            pltpu.VMEM(own, BF16),
            pltpu.VMEM((LANES, BS), BF16),
            pltpu.VMEM(own, BF16),
            pltpu.VMEM((LANES, LANES), BF16),
            pltpu.VMEM((LANES, LANES), BF16),
            dma, dma, dma,
            dma((SLOTS,)), dma((SLOTS,)),
            dma((SLOTS,)), dma((SIDE,)),
            dma((SLOTS,)), dma((SIDE,)),
            dma((SLOTS,)), dma((SIDE,)),
            dma((3, SIDE)), dma((3, SIDE)),
            dma((3, SIDE)), dma((3, SIDE)),
            dma((SIDE,)), dma((SLOTS,)),
            dma((SIDE,)), dma((SLOTS,)),
            dma((SIDE,)), dma((SLOTS,)),
            dma((SLOTS,)), dma((SLOTS,)),
        ],
        compiler_params=pltpu.CompilerParams(
            collective_id=0, has_side_effects=True, vmem_limit_bytes=60 * 1024 * 1024
        ),
    )(split, assignment, extents.T, root_left, root_right)
    new_left = BETA * factor_left + left_term.astype(F32)
    new_right = BETA * factor_right + right_term.astype(F32)
    line = jnp.arange(nblocks, dtype=jnp.int32)
    places = (line % SLOTS) * nf + line // SLOTS
    inverse = jnp.sum(jnp.where(assignment[None, :] == line[:, None], places[None, :], 0), axis=1)
    flat = ret.reshape(nblocks, BS // LANES, rpf, LANES).transpose(0, 2, 1, 3).reshape(nblocks, rpf, BS)
    update = flat.at[inverse].get(mode="promise_in_bounds").reshape(nblocks, 1, rpf, BS)
    return (update, new_left, new_right)


def solution(mesh):
    placed = (
        P(None, "rep", "fsdp", None),
        P(),
        P(),
        P("fsdp", "rep", None),
        P("fsdp", "rep", None),
        P("fsdp", "rep", None),
        P("fsdp", "rep", None),
    )
    return jax.shard_map(
        functools.partial(local, mesh.shape["fsdp"]),
        mesh=mesh,
        in_specs=placed,
        out_specs=(P(None, "rep", "fsdp", None), P("fsdp", "rep", None), P("fsdp", "rep", None)),
        check_vma=False,
    )
```

```python
import functools

import jax
import jax.numpy as jnp
from jax import lax
from jax.experimental import pallas as pl
from jax.experimental.pallas import tpu as pltpu
from jax.sharding import PartitionSpec as P

BETA = 0.95
MESH = pl.DeviceIdType.MESH
SIDE = 4
SLOTS = 3
RW = 64
BS = 1024
LANES = 128
F32 = jnp.float32
BF16 = jnp.bfloat16


def kernel(
    nf, grads, asg_in, ext_in, places_in, root_l, root_r, left_in, right_in, update_out, new_left, new_right,
    asg, ext, places, ret, left_out, right_out, factor_l, factor_r, grads_v, tiles, zin, fold_in, g_full, r_full, l_own, g_own, t_buf, u_buf, u_tiles, u_in, left_buf, right_buf, turned, g_cols,
    perm, perm_t,
    grads_sem, asg_sem, ext_sem, places_sem, factor_sem, z_send, z_recv, gf_send, gf_recv, rf_send, rf_recv, lf_send, lf_recv,
    ga_send, ga_recv, ra_send, ra_recv, u_send, u_recv, lo_send, lo_recv, ro_send, ro_recv, b_send, b_recv,
):
    me = lax.axis_index("fsdp")
    rep = lax.axis_index("rep")
    core = lax.rem(me, 2)
    y, x = rep // SIDE, lax.rem(rep, SIDE)
    fold = jnp.where(core == 0, y, x)
    ring = jnp.where(core == 0, x, y)
    fold_step = jnp.where(core == 0, SIDE, 1)
    ring_step = jnp.where(core == 0, 1, SIDE)

    def at(fold_pos, ring_pos):
        return fold_pos * fold_step + ring_pos * ring_step

    right = lax.rem(ring + 1, SIDE)
    left = lax.rem(ring + SIDE - 1, SIDE)
    across = lax.rem(ring + 2, SIDE)
    works = fold < SLOTS

    def remote(src, dst, ssem, rsem, fs, rp):
        return pltpu.make_async_remote_copy(
            src_ref=src, dst_ref=dst, send_sem=ssem, recv_sem=rsem, device_id=(fs, rp), device_id_type=MESH
        )

    def taken(ref, sem):
        pltpu.make_async_copy(ref, ref, sem).wait()

    staged = pltpu.make_async_copy(grads, grads_v, grads_sem)
    staged.start()
    numbers = pltpu.make_async_copy(asg_in, asg, asg_sem)
    numbers.start()
    limits = pltpu.make_async_copy(ext_in, ext, ext_sem)
    limits.start()
    order = pltpu.make_async_copy(places_in, places, places_sem)
    order.start()

    barrier = pltpu.get_barrier_semaphore()

    def greet(d, carry):
        pl.semaphore_signal(barrier, inc=1, device_id=(lax.rem(me + d, nf), rep), device_id_type=MESH)
        return carry

    for d in range(1, SIDE):
        pl.semaphore_signal(barrier, inc=1, device_id=(me, at(lax.rem(fold + d, SIDE), ring)), device_id_type=MESH)
    for pos in (left, right):
        pl.semaphore_signal(barrier, inc=1, device_id=(me, at(fold, pos)), device_id_type=MESH)
    lax.fori_loop(1, nf, greet, 0)
    pl.semaphore_wait(barrier, nf - 1 + SIDE - 1 + 2)

    def fold_root(root, place, sends, recvs):
        def push(s, carry):
            @pl.when(fold != s)
            def _():
                remote(root.at[s], place, sends.at[s], recvs.at[fold], me, at(s, ring)).start()

            @pl.when(fold == s)
            def _():
                pltpu.make_async_copy(root.at[s], place, recvs.at[fold]).start()

            return carry

        lax.fori_loop(0, SLOTS, push, 0)

    def other(i):
        half = (nf + 1 - i) // 2
        return lax.rem(me + jnp.where(lax.rem(i, 2) == 0, half, nf - half), nf)

    def send_tiles(s, carry):
        def push(i, carry):
            to = other(i)
            tiles[s, to] = grads_v[asg[to * SLOTS + s]]
            remote(tiles.at[s, to], zin.at[s, me], z_send.at[s], z_recv.at[s], to, rep).start()
            return carry

        lax.fori_loop(1, nf, push, 0)
        tiles[s, me] = grads_v[asg[me * SLOTS + s]]
        pltpu.make_async_copy(tiles.at[s, me], zin.at[s, me], z_recv.at[s]).start()
        return carry

    fold_root(root_r, r_full.at[rep], rf_send, rf_recv)
    staged.wait()
    numbers.wait()
    limits.wait()
    order.wait()
    lax.fori_loop(0, SLOTS, send_tiles, 0)
    fold_root(root_l, l_own.at[fold], lf_send, lf_recv)

    factors = [
        pltpu.make_async_copy(left_in, factor_l, factor_sem.at[0]),
        pltpu.make_async_copy(right_in, factor_r, factor_sem.at[1]),
    ]
    for copy in factors:
        copy.start()

    one = lax.broadcasted_iota(jnp.int32, (LANES, LANES), 0)
    two = lax.broadcasted_iota(jnp.int32, (LANES, LANES), 1)

    def tile_place(o):
        return (lax.rem(o, 16) // 2) * 16 + (o // 16) * 2 + lax.rem(o, 2)

    perm[...] = jnp.where(two == tile_place(one), 1.0, 0.0).astype(BF16)
    perm_t[...] = jnp.where(one == tile_place(two), 1.0, 0.0).astype(BF16)

    def spread(buf, sends, recvs, f):
        g = at(f, ring)
        remote(buf.at[g], buf.at[g], sends.at[0, f], recvs.at[0, f], me, at(fold, right)).start()
        remote(buf.at[g], buf.at[g], sends.at[1, f], recvs.at[1, f], me, at(fold, left)).start()

    def pass_on(buf, sends, recvs):
        def push(i, carry):
            way = lax.rem(i, 2)
            f = way * 2 + i // 2
            g = at(f, jnp.where(way == 0, left, right))
            taken(buf.at[g], recvs.at[way, f])
            to = at(fold, jnp.where(way == 0, right, left))
            remote(buf.at[g], buf.at[g], sends.at[2, f], recvs.at[2, f], me, to).start()
            return carry

        lax.fori_loop(0, SIDE, push, 0)

    def rest(buf, recvs):
        def await_piece(f, carry):
            way = 1 - f // 2
            taken(buf.at[at(f, jnp.where(way == 0, left, right))], recvs.at[way, f])
            taken(buf.at[at(f, across)], recvs.at[2, f])
            return carry

        lax.fori_loop(0, SIDE, await_piece, 0)

    slot = me * SLOTS + jnp.minimum(fold, SLOTS - 1)
    block = asg[slot]
    rows_ok = ext[0, block]
    cols_ok = ext[1, block]

    def unpack(i, carry):
        f = lax.rem(fold + i, SIDE)
        taken(fold_in.at[f], gf_recv.at[f])
        g = at(f, ring)
        groups = [fold_in[f, q * 8 : (q + 1) * 8].reshape(LANES, LANES) for q in range(4)]
        flat = jnp.dot(perm[...], jnp.concatenate(groups, axis=1), preferred_element_type=F32)
        row_ids = g * RW + lax.broadcasted_iota(jnp.int32, (16, LANES), 0)
        col_ids = lax.broadcasted_iota(jnp.int32, (16, LANES), 1)
        for q in range(4):
            for c in range(BS // LANES):
                ok = jnp.logical_and(row_ids + q * 16 < rows_ok, col_ids + c * LANES < cols_ok)
                part = flat[c * 16 : (c + 1) * 16, q * LANES : (q + 1) * LANES]
                part = jnp.where(ok, part, 0.0).astype(BF16)
                g_full[g, q * 16 : (q + 1) * 16, c * LANES : (c + 1) * LANES] = part
                g_own[f, q * 16 : (q + 1) * 16, c * LANES : (c + 1) * LANES] = part
        spread(g_full, ga_send, ga_recv, f)
        return carry

    own_rows = SIDE * RW

    def update_part():
        rest(g_full, ga_recv)

        def await_left(f, carry):
            taken(l_own.at[f], lf_recv.at[f])
            return carry

        lax.fori_loop(0, SIDE, await_left, 0)
        t_buf[...] = jnp.dot(
            l_own[...].reshape(own_rows, BS), g_full[...].reshape(BS, BS), preferred_element_type=F32
        ).astype(BF16)
        rest(r_full, ra_recv)
        u = jnp.dot(t_buf[...], r_full[...].reshape(BS, BS), preferred_element_type=F32)
        col_ids = lax.broadcasted_iota(jnp.int32, (RW, BS), 1)
        for f in range(SIDE):
            row_ids = at(f, ring) * RW + lax.broadcasted_iota(jnp.int32, (RW, BS), 0)
            ok = jnp.logical_and(row_ids < rows_ok, col_ids < cols_ok)
            u_buf[f * RW : (f + 1) * RW, :] = jnp.where(ok, u[f * RW : (f + 1) * RW, :], 0.0).astype(BF16)

        def pack(i, carry):
            f = lax.rem(fold + 1 + i, SIDE)
            rows = u_buf[pl.ds(pl.multiple_of(f * RW, RW), RW), :]
            groups = [
                jnp.concatenate(
                    [rows[q * 16 : (q + 1) * 16, c * LANES : (c + 1) * LANES] for c in range(BS // LANES)], axis=0
                )
                for q in range(4)
            ]
            flat = jnp.dot(perm_t[...], jnp.concatenate(groups, axis=1), preferred_element_type=F32).astype(BF16)
            for q in range(4):
                u_tiles[f, q * 8 : (q + 1) * 8] = flat[:, q * LANES : (q + 1) * LANES].reshape(8, 16, LANES)

            @pl.when(fold != f)
            def _():
                remote(u_tiles.at[f], u_in.at[fold], u_send.at[f], u_recv.at[fold], me, at(f, ring)).start()

            @pl.when(fold == f)
            def _():
                pltpu.make_async_copy(u_tiles.at[f], u_in.at[fold], u_recv.at[fold]).start()

            return carry

        lax.fori_loop(0, SIDE, pack, 0)

    def factor_part():
        part = lax.dot_general(
            g_own[...].reshape(own_rows, BS),
            g_full[...].reshape(BS, BS),
            (((1,), (1,)), ((), ())),
            preferred_element_type=F32,
        )
        left_buf[...] = ((1.0 - BETA) * part).astype(BF16).reshape(SIDE, RW, BS)

        def home(buf, out, sends, recvs, f):
            @pl.when(fold != f)
            def _():
                remote(buf.at[f], out.at[fold], sends.at[f], recvs.at[fold], me, at(f, ring)).start()

            @pl.when(fold == f)
            def _():
                pltpu.make_async_copy(buf.at[f], out.at[fold], recvs.at[fold]).start()

        def left_home(f, carry):
            home(left_buf, left_out, lo_send, lo_recv, f)
            return carry

        lax.fori_loop(0, SIDE, left_home, 0)

        def own_columns(f, carry):
            g = at(f, ring)
            pair = pl.ds(pl.multiple_of((g // 2) * LANES, LANES), LANES)
            turned[...] = g_full[:, :, pair].reshape(BS, LANES).T
            g_cols[f] = turned[pl.ds(pl.multiple_of(lax.rem(g, 2) * RW, RW), RW), :]
            return carry

        lax.fori_loop(0, SIDE, own_columns, 0)
        part = jnp.dot(g_cols[...].reshape(own_rows, BS), g_full[...].reshape(BS, BS), preferred_element_type=F32)
        right_buf[...] = ((1.0 - BETA) * part).astype(BF16).reshape(SIDE, RW, BS)

        def right_home(f, carry):
            home(right_buf, right_out, ro_send, ro_recv, f)
            return carry

        lax.fori_loop(0, SIDE, right_home, 0)

    def send_back(s):
        taken(u_in.at[s], u_recv.at[s])

        def push_back(i, carry):
            to = other(i)
            remote(u_in.at[s, to], ret.at[s, me], b_send.at[s], b_recv.at[s], to, rep).start()
            return carry

        lax.fori_loop(1, nf, push_back, 0)
        pltpu.make_async_copy(u_in.at[s, me], ret.at[s, me], b_recv.at[s]).start()

    @pl.when(works)
    def _():
        def root_piece(f, carry):
            taken(r_full.at[at(f, ring)], rf_recv.at[f])
            spread(r_full, ra_send, ra_recv, f)
            return carry

        lax.fori_loop(0, SIDE, root_piece, 0)

    def fold_tiles(s, carry):
        taken(zin.at[s], z_recv.at[s])

        @pl.when(fold != s)
        def _():
            remote(zin.at[s], fold_in.at[fold], gf_send.at[s], gf_recv.at[fold], me, at(s, ring)).start()

        @pl.when(fold == s)
        def _():
            pltpu.make_async_copy(zin.at[s], fold_in.at[fold], gf_recv.at[fold]).start()
            lax.fori_loop(0, SIDE, unpack, 0)

        @pl.when(jnp.logical_and(works, s == 0))
        def _():
            pass_on(r_full, ra_send, ra_recv)

        return carry

    lax.fori_loop(0, SLOTS, fold_tiles, 0)

    @pl.when(works)
    def _():
        pass_on(g_full, ga_send, ga_recv)

    def turn(s, carry):
        @pl.when(jnp.logical_and(works, s == jnp.maximum(fold - 1, 0)))
        def _():
            update_part()

        send_back(s)
        pl.when(fold == s)(factor_part)
        return carry

    lax.fori_loop(0, SLOTS, turn, 0)

    for copy in factors:
        copy.wait()

    def new_factors(s, carry):
        taken(left_out.at[s], lo_recv.at[s])
        new_left[s] = BETA * factor_l[s] + left_out[s].astype(F32)
        taken(right_out.at[s], ro_recv.at[s])
        new_right[s] = BETA * factor_r[s] + right_out[s].astype(F32)
        return carry

    lax.fori_loop(0, SLOTS, new_factors, 0)

    def returned(s, carry):
        taken(ret.at[s], b_recv.at[s])
        return carry

    lax.fori_loop(0, SLOTS, returned, 0)

    def block_order(b, carry):
        place = places[b]
        update_out[b] = ret[place // nf, lax.rem(place, nf)]
        return carry

    lax.fori_loop(0, nf * SLOTS, block_order, 0, unroll=4)

    def finish(s, carry):
        taken(tiles.at[s, pl.ds(0, nf - 1)], z_send.at[s])
        taken(u_in.at[s, pl.ds(0, nf - 1)], b_send.at[s])

        @pl.when(fold != s)
        def _():
            taken(zin.at[s], gf_send.at[s])
            taken(root_r.at[s], rf_send.at[s])
            taken(root_l.at[s], lf_send.at[s])

        return carry

    lax.fori_loop(0, SLOTS, finish, 0)

    @pl.when(works)
    def _():
        def sent(f, carry):
            for way in range(3):
                taken(g_full.at[f], ga_send.at[way, f])
                taken(r_full.at[f], ra_send.at[way, f])

            @pl.when(fold != f)
            def _():
                taken(u_tiles.at[f], u_send.at[f])
                taken(left_buf.at[f], lo_send.at[f])
                taken(right_buf.at[f], ro_send.at[f])

            return carry

        lax.fori_loop(0, SIDE, sent, 0)

def local(nf, grads, assignment, extents, factor_left, factor_right, root_left, root_right):
    nblocks = assignment.shape[0]
    rpf = RW // nf
    tile_rows = rpf * BS // LANES
    split = grads.reshape(nblocks, rpf, BS // LANES, LANES).transpose(0, 2, 1, 3).reshape(nblocks, tile_rows, LANES)
    dma = pltpu.SemaphoreType.DMA
    vmem = pl.BlockSpec(memory_space=pltpu.VMEM)
    hbm = pl.BlockSpec(memory_space=pltpu.HBM)
    rows = (SLOTS, RW, BS)
    own = (SIDE, RW, BS)
    line = jnp.arange(nblocks, dtype=jnp.int32)
    slot_places = (line % SLOTS) * nf + line // SLOTS
    places = jnp.sum(jnp.where(assignment[None, :] == line[:, None], slot_places[None, :], 0), axis=1)
    update, new_left, new_right = pl.pallas_call(
        functools.partial(kernel, nf),
        out_shape=(
            pltpu.VMEM((nblocks, tile_rows, LANES), BF16),
            pltpu.VMEM(rows, F32),
            pltpu.VMEM(rows, F32),
        ),
        in_specs=[hbm] * 8,
        out_specs=(vmem, vmem, vmem),
        scratch_shapes=[
            pltpu.SMEM((nblocks,), jnp.int32),
            pltpu.SMEM((2, nblocks), jnp.int32),
            pltpu.SMEM((nblocks,), jnp.int32),
            pltpu.VMEM((SLOTS, nf, tile_rows, LANES), BF16),
            pltpu.VMEM(rows, BF16),
            pltpu.VMEM(rows, BF16),
            pltpu.VMEM(rows, F32),
            pltpu.VMEM(rows, F32),
            pltpu.VMEM((nblocks, tile_rows, LANES), BF16),
            pltpu.VMEM((SLOTS, nf, tile_rows, LANES), BF16),
            pltpu.VMEM((SLOTS, nf, tile_rows, LANES), BF16),
            pltpu.VMEM((SIDE, nf, tile_rows, LANES), BF16),
            pltpu.VMEM((SIDE * SIDE, RW, BS), BF16),
            pltpu.VMEM((SIDE * SIDE, RW, BS), BF16),
            pltpu.VMEM(own, BF16),
            pltpu.VMEM(own, BF16),
            pltpu.VMEM((SIDE * RW, BS), BF16),
            pltpu.VMEM((SIDE * RW, BS), BF16),
            pltpu.VMEM((SIDE, nf, tile_rows, LANES), BF16),
            pltpu.VMEM((SLOTS, nf, tile_rows, LANES), BF16),
            pltpu.VMEM(own, BF16),
            pltpu.VMEM(own, BF16),
            pltpu.VMEM((LANES, BS), BF16),
            pltpu.VMEM(own, BF16),
            pltpu.VMEM((LANES, LANES), BF16),
            pltpu.VMEM((LANES, LANES), BF16),
            dma, dma, dma, dma,
            dma((2,)),
            dma((SLOTS,)), dma((SLOTS,)),
            dma((SLOTS,)), dma((SIDE,)),
            dma((SLOTS,)), dma((SIDE,)),
            dma((SLOTS,)), dma((SIDE,)),
            dma((3, SIDE)), dma((3, SIDE)),
            dma((3, SIDE)), dma((3, SIDE)),
            dma((SIDE,)), dma((SLOTS,)),
            dma((SIDE,)), dma((SLOTS,)),
            dma((SIDE,)), dma((SLOTS,)),
            dma((SLOTS,)), dma((SLOTS,)),
        ],
        compiler_params=pltpu.CompilerParams(
            collective_id=0, has_side_effects=True, vmem_limit_bytes=56 * 1024 * 1024
        ),
    )(split, assignment, extents.T, places, root_left, root_right, factor_left, factor_right)
    update = update.reshape(nblocks, BS // LANES, rpf, LANES).transpose(0, 2, 1, 3).reshape(nblocks, 1, rpf, BS)
    return (update, new_left, new_right)


def solution(mesh):
    placed = (
        P(None, "rep", "fsdp", None),
        P(),
        P(),
        P("fsdp", "rep", None),
        P("fsdp", "rep", None),
        P("fsdp", "rep", None),
        P("fsdp", "rep", None),
    )
    return jax.shard_map(
        functools.partial(local, mesh.shape["fsdp"]),
        mesh=mesh,
        in_specs=placed,
        out_specs=(P(None, "rep", "fsdp", None), P("fsdp", "rep", None), P("fsdp", "rep", None)),
        check_vma=False,
    )
```

```python
import functools

import jax
import jax.numpy as jnp
from jax import lax
from jax.experimental import pallas as pl
from jax.experimental.pallas import tpu as pltpu
from jax.sharding import PartitionSpec as P

BETA = 0.95
MESH = pl.DeviceIdType.MESH
SIDE = 4
SLOTS = 3
RW = 64
BS = 1024
LANES = 128
F32 = jnp.float32
BF16 = jnp.bfloat16


def kernel(
    nf, grads, asg_in, ext_in, root_l, root_r, left_in, right_in, update_out, new_left, new_right,
    asg, ext, places, places_v, ret, left_out, right_out, factor_l, factor_r, grads_v, tiles, zin, fold_in, g_full, r_full, l_own, g_own, t_buf, u_buf, u_tiles, u_in, left_buf, right_buf, turned, g_cols,
    perm, perm_t,
    grads_sem, asg_sem, ext_sem, places_sem, factor_sem, z_send, z_recv, gf_send, gf_recv, rf_send, rf_recv, lf_send, lf_recv,
    ga_send, ga_recv, ra_send, ra_recv, u_send, u_recv, lo_send, lo_recv, ro_send, ro_recv, b_send, b_recv,
):
    me = lax.axis_index("fsdp")
    rep = lax.axis_index("rep")
    core = lax.rem(me, 2)
    y, x = rep // SIDE, lax.rem(rep, SIDE)
    fold = jnp.where(core == 0, y, x)
    ring = jnp.where(core == 0, x, y)
    fold_step = jnp.where(core == 0, SIDE, 1)
    ring_step = jnp.where(core == 0, 1, SIDE)

    def at(fold_pos, ring_pos):
        return fold_pos * fold_step + ring_pos * ring_step

    right = lax.rem(ring + 1, SIDE)
    left = lax.rem(ring + SIDE - 1, SIDE)
    across = lax.rem(ring + 2, SIDE)
    works = fold < SLOTS

    def remote(src, dst, ssem, rsem, fs, rp):
        return pltpu.make_async_remote_copy(
            src_ref=src, dst_ref=dst, send_sem=ssem, recv_sem=rsem, device_id=(fs, rp), device_id_type=MESH
        )

    def taken(ref, sem):
        pltpu.make_async_copy(ref, ref, sem).wait()

    staged = pltpu.make_async_copy(grads, grads_v, grads_sem)
    staged.start()
    numbers = pltpu.make_async_copy(asg_in, asg, asg_sem)
    numbers.start()
    limits = pltpu.make_async_copy(ext_in, ext, ext_sem)
    limits.start()

    barrier = pltpu.get_barrier_semaphore()

    def greet(d, carry):
        pl.semaphore_signal(barrier, inc=1, device_id=(lax.rem(me + d, nf), rep), device_id_type=MESH)
        return carry

    for d in range(1, SIDE):
        pl.semaphore_signal(barrier, inc=1, device_id=(me, at(lax.rem(fold + d, SIDE), ring)), device_id_type=MESH)
    for pos in (left, right):
        pl.semaphore_signal(barrier, inc=1, device_id=(me, at(fold, pos)), device_id_type=MESH)
    lax.fori_loop(1, nf, greet, 0)
    pl.semaphore_wait(barrier, nf - 1 + SIDE - 1 + 2)

    def fold_root(root, place, sends, recvs):
        def push(s, carry):
            @pl.when(fold != s)
            def _():
                remote(root.at[s], place, sends.at[s], recvs.at[fold], me, at(s, ring)).start()

            @pl.when(fold == s)
            def _():
                pltpu.make_async_copy(root.at[s], place, recvs.at[fold]).start()

            return carry

        lax.fori_loop(0, SLOTS, push, 0)

    def other(i):
        half = (nf + 1 - i) // 2
        return lax.rem(me + jnp.where(lax.rem(i, 2) == 0, half, nf - half), nf)

    def send_tiles(s, carry):
        def push(i, carry):
            to = other(i)
            tiles[s, to] = grads_v[asg[to * SLOTS + s]]
            remote(tiles.at[s, to], zin.at[s, me], z_send.at[s], z_recv.at[s], to, rep).start()
            return carry

        lax.fori_loop(1, nf, push, 0)
        tiles[s, me] = grads_v[asg[me * SLOTS + s]]
        pltpu.make_async_copy(tiles.at[s, me], zin.at[s, me], z_recv.at[s]).start()
        return carry

    fold_root(root_r, r_full.at[rep], rf_send, rf_recv)
    staged.wait()
    numbers.wait()
    limits.wait()
    lax.fori_loop(0, SLOTS, send_tiles, 0)
    fold_root(root_l, l_own.at[fold], lf_send, lf_recv)

    factors = [
        pltpu.make_async_copy(left_in, factor_l, factor_sem.at[0]),
        pltpu.make_async_copy(right_in, factor_r, factor_sem.at[1]),
    ]
    for copy in factors:
        copy.start()

    one = lax.broadcasted_iota(jnp.int32, (LANES, LANES), 0)
    two = lax.broadcasted_iota(jnp.int32, (LANES, LANES), 1)

    def tile_place(o):
        return (lax.rem(o, 16) // 2) * 16 + (o // 16) * 2 + lax.rem(o, 2)

    perm[...] = jnp.where(two == tile_place(one), 1.0, 0.0).astype(BF16)
    perm_t[...] = jnp.where(one == tile_place(two), 1.0, 0.0).astype(BF16)

    def spread(buf, sends, recvs, f):
        g = at(f, ring)
        remote(buf.at[g], buf.at[g], sends.at[0, f], recvs.at[0, f], me, at(fold, right)).start()
        remote(buf.at[g], buf.at[g], sends.at[1, f], recvs.at[1, f], me, at(fold, left)).start()

    def pass_on(buf, sends, recvs):
        def push(i, carry):
            way = lax.rem(i, 2)
            f = way * 2 + i // 2
            g = at(f, jnp.where(way == 0, left, right))
            taken(buf.at[g], recvs.at[way, f])
            to = at(fold, jnp.where(way == 0, right, left))
            remote(buf.at[g], buf.at[g], sends.at[2, f], recvs.at[2, f], me, to).start()
            return carry

        lax.fori_loop(0, SIDE, push, 0)

    def rest(buf, recvs):
        def await_piece(f, carry):
            way = 1 - f // 2
            taken(buf.at[at(f, jnp.where(way == 0, left, right))], recvs.at[way, f])
            taken(buf.at[at(f, across)], recvs.at[2, f])
            return carry

        lax.fori_loop(0, SIDE, await_piece, 0)

    slot = me * SLOTS + jnp.minimum(fold, SLOTS - 1)
    block = asg[slot]
    rows_ok = ext[0, block]
    cols_ok = ext[1, block]

    def unpack(i, carry):
        f = lax.rem(fold + i, SIDE)
        taken(fold_in.at[f], gf_recv.at[f])
        g = at(f, ring)
        groups = [fold_in[f, q * 8 : (q + 1) * 8].reshape(LANES, LANES) for q in range(4)]
        flat = jnp.dot(perm[...], jnp.concatenate(groups, axis=1), preferred_element_type=F32)
        row_ids = g * RW + lax.broadcasted_iota(jnp.int32, (16, LANES), 0)
        col_ids = lax.broadcasted_iota(jnp.int32, (16, LANES), 1)
        for q in range(4):
            for c in range(BS // LANES):
                ok = jnp.logical_and(row_ids + q * 16 < rows_ok, col_ids + c * LANES < cols_ok)
                part = flat[c * 16 : (c + 1) * 16, q * LANES : (q + 1) * LANES]
                part = jnp.where(ok, part, 0.0).astype(BF16)
                g_full[g, q * 16 : (q + 1) * 16, c * LANES : (c + 1) * LANES] = part
                g_own[f, q * 16 : (q + 1) * 16, c * LANES : (c + 1) * LANES] = part
        spread(g_full, ga_send, ga_recv, f)
        return carry

    own_rows = SIDE * RW

    def update_part():
        rest(g_full, ga_recv)

        def await_left(f, carry):
            taken(l_own.at[f], lf_recv.at[f])
            return carry

        lax.fori_loop(0, SIDE, await_left, 0)
        t_buf[...] = jnp.dot(
            l_own[...].reshape(own_rows, BS), g_full[...].reshape(BS, BS), preferred_element_type=F32
        ).astype(BF16)
        rest(r_full, ra_recv)
        u = jnp.dot(t_buf[...], r_full[...].reshape(BS, BS), preferred_element_type=F32)
        col_ids = lax.broadcasted_iota(jnp.int32, (RW, BS), 1)
        for f in range(SIDE):
            row_ids = at(f, ring) * RW + lax.broadcasted_iota(jnp.int32, (RW, BS), 0)
            ok = jnp.logical_and(row_ids < rows_ok, col_ids < cols_ok)
            u_buf[f * RW : (f + 1) * RW, :] = jnp.where(ok, u[f * RW : (f + 1) * RW, :], 0.0).astype(BF16)

        def pack(i, carry):
            f = lax.rem(fold + 1 + i, SIDE)
            rows = u_buf[pl.ds(pl.multiple_of(f * RW, RW), RW), :]
            groups = [
                jnp.concatenate(
                    [rows[q * 16 : (q + 1) * 16, c * LANES : (c + 1) * LANES] for c in range(BS // LANES)], axis=0
                )
                for q in range(4)
            ]
            flat = jnp.dot(perm_t[...], jnp.concatenate(groups, axis=1), preferred_element_type=F32).astype(BF16)
            for q in range(4):
                u_tiles[f, q * 8 : (q + 1) * 8] = flat[:, q * LANES : (q + 1) * LANES].reshape(8, 16, LANES)

            @pl.when(fold != f)
            def _():
                remote(u_tiles.at[f], u_in.at[fold], u_send.at[f], u_recv.at[fold], me, at(f, ring)).start()

            @pl.when(fold == f)
            def _():
                pltpu.make_async_copy(u_tiles.at[f], u_in.at[fold], u_recv.at[fold]).start()

            return carry

        lax.fori_loop(0, SIDE, pack, 0)

    def factor_part():
        part = lax.dot_general(
            g_own[...].reshape(own_rows, BS),
            g_full[...].reshape(BS, BS),
            (((1,), (1,)), ((), ())),
            preferred_element_type=F32,
        )
        left_buf[...] = ((1.0 - BETA) * part).astype(BF16).reshape(SIDE, RW, BS)

        def home(buf, out, sends, recvs, f):
            @pl.when(fold != f)
            def _():
                remote(buf.at[f], out.at[fold], sends.at[f], recvs.at[fold], me, at(f, ring)).start()

            @pl.when(fold == f)
            def _():
                pltpu.make_async_copy(buf.at[f], out.at[fold], recvs.at[fold]).start()

        def left_home(f, carry):
            home(left_buf, left_out, lo_send, lo_recv, f)
            return carry

        lax.fori_loop(0, SIDE, left_home, 0)

        def own_columns(f, carry):
            g = at(f, ring)
            pair = pl.ds(pl.multiple_of((g // 2) * LANES, LANES), LANES)
            turned[...] = g_full[:, :, pair].reshape(BS, LANES).T
            g_cols[f] = turned[pl.ds(pl.multiple_of(lax.rem(g, 2) * RW, RW), RW), :]
            return carry

        lax.fori_loop(0, SIDE, own_columns, 0)
        part = jnp.dot(g_cols[...].reshape(own_rows, BS), g_full[...].reshape(BS, BS), preferred_element_type=F32)
        right_buf[...] = ((1.0 - BETA) * part).astype(BF16).reshape(SIDE, RW, BS)

        def right_home(f, carry):
            home(right_buf, right_out, ro_send, ro_recv, f)
            return carry

        lax.fori_loop(0, SIDE, right_home, 0)

    def send_back(s):
        taken(u_in.at[s], u_recv.at[s])

        def push_back(i, carry):
            to = other(i)
            remote(u_in.at[s, to], ret.at[s, me], b_send.at[s], b_recv.at[s], to, rep).start()
            return carry

        lax.fori_loop(1, nf, push_back, 0)
        pltpu.make_async_copy(u_in.at[s, me], ret.at[s, me], b_recv.at[s]).start()

    @pl.when(works)
    def _():
        def root_piece(f, carry):
            taken(r_full.at[at(f, ring)], rf_recv.at[f])
            spread(r_full, ra_send, ra_recv, f)
            return carry

        lax.fori_loop(0, SIDE, root_piece, 0)

    lanes = lax.broadcasted_iota(jnp.int32, (8, LANES), 1)

    def place_of(k, found):
        return jnp.where(lanes == asg[k], lax.rem(k, SLOTS) * nf + k // SLOTS, found)

    places_v[...] = lax.fori_loop(0, nf * SLOTS, place_of, jnp.zeros((8, LANES), jnp.int32))
    order = pltpu.make_async_copy(places_v, places, places_sem)
    order.start()

    def fold_tiles(s, carry):
        taken(zin.at[s], z_recv.at[s])

        @pl.when(fold != s)
        def _():
            remote(zin.at[s], fold_in.at[fold], gf_send.at[s], gf_recv.at[fold], me, at(s, ring)).start()

        @pl.when(fold == s)
        def _():
            pltpu.make_async_copy(zin.at[s], fold_in.at[fold], gf_recv.at[fold]).start()
            lax.fori_loop(0, SIDE, unpack, 0)

        @pl.when(jnp.logical_and(works, s == 0))
        def _():
            pass_on(r_full, ra_send, ra_recv)

        return carry

    lax.fori_loop(0, SLOTS, fold_tiles, 0)

    @pl.when(works)
    def _():
        pass_on(g_full, ga_send, ga_recv)

    def turn(s, carry):
        @pl.when(jnp.logical_and(works, s == jnp.maximum(fold - 1, 0)))
        def _():
            update_part()

        send_back(s)
        pl.when(fold == s)(factor_part)
        return carry

    lax.fori_loop(0, SLOTS, turn, 0)

    for copy in factors:
        copy.wait()

    def new_factors(s, carry):
        taken(left_out.at[s], lo_recv.at[s])
        new_left[s] = BETA * factor_l[s] + left_out[s].astype(F32)
        taken(right_out.at[s], ro_recv.at[s])
        new_right[s] = BETA * factor_r[s] + right_out[s].astype(F32)
        return carry

    lax.fori_loop(0, SLOTS, new_factors, 0)

    def returned(s, carry):
        taken(ret.at[s], b_recv.at[s])
        return carry

    lax.fori_loop(0, SLOTS, returned, 0)

    order.wait()

    def block_order(b, carry):
        place = places[0, b]
        update_out[b] = ret[place // nf, lax.rem(place, nf)]
        return carry

    lax.fori_loop(0, nf * SLOTS, block_order, 0, unroll=4)

    def finish(s, carry):
        taken(tiles.at[s, pl.ds(0, nf - 1)], z_send.at[s])
        taken(u_in.at[s, pl.ds(0, nf - 1)], b_send.at[s])

        @pl.when(fold != s)
        def _():
            taken(zin.at[s], gf_send.at[s])
            taken(root_r.at[s], rf_send.at[s])
            taken(root_l.at[s], lf_send.at[s])

        return carry

    lax.fori_loop(0, SLOTS, finish, 0)

    @pl.when(works)
    def _():
        def sent(f, carry):
            for way in range(3):
                taken(g_full.at[f], ga_send.at[way, f])
                taken(r_full.at[f], ra_send.at[way, f])

            @pl.when(fold != f)
            def _():
                taken(u_tiles.at[f], u_send.at[f])
                taken(left_buf.at[f], lo_send.at[f])
                taken(right_buf.at[f], ro_send.at[f])

            return carry

        lax.fori_loop(0, SIDE, sent, 0)

def local(nf, grads, assignment, extents, factor_left, factor_right, root_left, root_right):
    nblocks = assignment.shape[0]
    rpf = RW // nf
    tile_rows = rpf * BS // LANES
    split = grads.reshape(nblocks, rpf, BS // LANES, LANES).transpose(0, 2, 1, 3).reshape(nblocks, tile_rows, LANES)
    dma = pltpu.SemaphoreType.DMA
    vmem = pl.BlockSpec(memory_space=pltpu.VMEM)
    hbm = pl.BlockSpec(memory_space=pltpu.HBM)
    rows = (SLOTS, RW, BS)
    own = (SIDE, RW, BS)
    update, new_left, new_right = pl.pallas_call(
        functools.partial(kernel, nf),
        out_shape=(
            pltpu.VMEM((nblocks, tile_rows, LANES), BF16),
            pltpu.VMEM(rows, F32),
            pltpu.VMEM(rows, F32),
        ),
        in_specs=[hbm] * 7,
        out_specs=(vmem, vmem, vmem),
        scratch_shapes=[
            pltpu.SMEM((nblocks,), jnp.int32),
            pltpu.SMEM((2, nblocks), jnp.int32),
            pltpu.SMEM((8, LANES), jnp.int32),
            pltpu.VMEM((8, LANES), jnp.int32),
            pltpu.VMEM((SLOTS, nf, tile_rows, LANES), BF16),
            pltpu.VMEM(rows, BF16),
            pltpu.VMEM(rows, BF16),
            pltpu.VMEM(rows, F32),
            pltpu.VMEM(rows, F32),
            pltpu.VMEM((nblocks, tile_rows, LANES), BF16),
            pltpu.VMEM((SLOTS, nf, tile_rows, LANES), BF16),
            pltpu.VMEM((SLOTS, nf, tile_rows, LANES), BF16),
            pltpu.VMEM((SIDE, nf, tile_rows, LANES), BF16),
            pltpu.VMEM((SIDE * SIDE, RW, BS), BF16),
            pltpu.VMEM((SIDE * SIDE, RW, BS), BF16),
            pltpu.VMEM(own, BF16),
            pltpu.VMEM(own, BF16),
            pltpu.VMEM((SIDE * RW, BS), BF16),
            pltpu.VMEM((SIDE * RW, BS), BF16),
            pltpu.VMEM((SIDE, nf, tile_rows, LANES), BF16),
            pltpu.VMEM((SLOTS, nf, tile_rows, LANES), BF16),
            pltpu.VMEM(own, BF16),
            pltpu.VMEM(own, BF16),
            pltpu.VMEM((LANES, BS), BF16),
            pltpu.VMEM(own, BF16),
            pltpu.VMEM((LANES, LANES), BF16),
            pltpu.VMEM((LANES, LANES), BF16),
            dma, dma, dma, dma,
            dma((2,)),
            dma((SLOTS,)), dma((SLOTS,)),
            dma((SLOTS,)), dma((SIDE,)),
            dma((SLOTS,)), dma((SIDE,)),
            dma((SLOTS,)), dma((SIDE,)),
            dma((3, SIDE)), dma((3, SIDE)),
            dma((3, SIDE)), dma((3, SIDE)),
            dma((SIDE,)), dma((SLOTS,)),
            dma((SIDE,)), dma((SLOTS,)),
            dma((SIDE,)), dma((SLOTS,)),
            dma((SLOTS,)), dma((SLOTS,)),
        ],
        compiler_params=pltpu.CompilerParams(
            collective_id=0, has_side_effects=True, vmem_limit_bytes=56 * 1024 * 1024
        ),
    )(split, assignment, extents.T, root_left, root_right, factor_left, factor_right)
    update = update.reshape(nblocks, BS // LANES, rpf, LANES).transpose(0, 2, 1, 3).reshape(nblocks, 1, rpf, BS)
    return (update, new_left, new_right)


def solution(mesh):
    placed = (
        P(None, "rep", "fsdp", None),
        P(),
        P(),
        P("fsdp", "rep", None),
        P("fsdp", "rep", None),
        P("fsdp", "rep", None),
        P("fsdp", "rep", None),
    )
    return jax.shard_map(
        functools.partial(local, mesh.shape["fsdp"]),
        mesh=mesh,
        in_specs=placed,
        out_specs=(P(None, "rep", "fsdp", None), P("fsdp", "rep", None), P("fsdp", "rep", None)),
        check_vma=False,
    )
```
